32 devices in a mesh: batch: 8 (over z, y), proto: 4 (over x, core).
Axes of the slice: x: 2, y: 2, z: 4, core: 2. Of those that a mesh axis runs over, the one named last changes fastest.
Arguments:
- features: bfloat16 [4096, 2048], P(('batch', 'proto')), may hold values from -6 to 6
- w_first: bfloat16 [2048, 2048], replicated, may hold values from -0.125 to 0.125
- bn_gain: float32 [2048], replicated, may hold values from 0.1 to 1.9
- bn_bias: float32 [2048], replicated, may hold values from -3 to 3
- w_second: bfloat16 [2048, 256], replicated, may hold values from -0.125 to 0.125
- prototypes: bfloat16 [16384, 256], P('proto'), may hold values from -16 to 16
- pair: int32 [4096], P('batch'), may hold values from 0 to 4095, as said below
Outputs:
- grad_first: float32 [2048, 2048], P(('batch', 'proto'))
- grad_second: float32 [2048, 256], P(('batch', 'proto'))
- grad_gain: float32 [2048], replicated
- grad_bias: float32 [2048], replicated
- grad_proto: float32 [16384, 256], P('proto', 'batch')
- loss: float32 [], replicated
The draws below stay inside these ranges and needn't reach their ends.
Inputs may be any that keep to these rules, and one draw needn't show every extreme that they name: pair is an involution without fixed points: pair[pair[i]] = i and pair[i] != i, and rows i and pair[i] lie in the same aligned block of 512 rows.
All inputs are finite; a program needn't handle non-finite values.
Results may differ from the reference program's by a relative error of at most 0.015.
Values may be sent and summed in bfloat16 or wider, within the bound.
A program may use at most 128 MiB of HBM per device.

```python
import jax
import jax.numpy as jnp
from jax import lax

D_IN = 2048
HIDDEN_SIZE = 2048
EMBED = 256
PROTOS = 16384
ITERS = 3
ROWS = 4096
GROUP_ROWS = 512
N_BATCH = 8
N_PROTO = 4


def draw_pair(key, part):
    blocks = ROWS // GROUP_ROWS
    block_keys = jax.random.split(jax.random.fold_in(key, 17), blocks)
    shuffled = jax.vmap(lambda block_key: jax.random.permutation(block_key, GROUP_ROWS))(block_keys).astype(jnp.int32)
    positions = jnp.arange(GROUP_ROWS, dtype=jnp.int32)
    partner_slot = jnp.bitwise_xor(positions, 1)

    def invert_block(permuted):
        return jnp.zeros((GROUP_ROWS,), jnp.int32).at[permuted].set(permuted[partner_slot])
    in_block = jax.vmap(invert_block)(shuffled)
    offsets = (jnp.arange(blocks, dtype=jnp.int32) * GROUP_ROWS)[:, None]
    return (in_block + offsets).reshape(ROWS)


def draw_prototypes(key, part):
    noise_key = jax.random.fold_in(key, 31)
    center_key = jax.random.fold_in(key, 43)
    centers = jnp.clip(jax.random.normal(center_key, (N_PROTO, EMBED), jnp.float32), -4.0, 4.0)
    position = jnp.arange(PROTOS, dtype=jnp.int32)
    group_index = position * N_PROTO // PROTOS
    chosen = jnp.take(centers, group_index, axis=0)
    fraction = position.astype(jnp.float32) / PROTOS
    noise = jnp.clip(jax.random.normal(noise_key, (PROTOS, EMBED), jnp.float32), -6.0, 6.0)
    strength = 0.6 + 1.8 * fraction
    return (noise + strength[:, None] * chosen).astype(jnp.bfloat16)


def with_spikes(values, stream_key, source, target, shards_of, factor):
    def block_of(axis_at):
        return (jnp.arange(values.shape[axis_at]) // (values.shape[axis_at] // shards_of)).reshape((-1,) + (1,) * (values.ndim - 1 - axis_at))

    near = jax.random.permutation(stream_key, shards_of)[block_of(target)]
    far = (block_of(target) + shards_of // 2) % shards_of
    return jnp.where((block_of(source) == near) | (block_of(source) == far), factor * values, values)


def shard_levels(stream_key, extent, cuts, least, largest):
    factor_of, own = 1.0, jax.random.fold_in(stream_key, 6)
    for dim, shards_of in cuts:
        steps = jnp.exp(jax.random.uniform(jax.random.fold_in(own, dim), (shards_of,), jnp.float32, least / len(cuts), largest / len(cuts)))
        factor_of = factor_of * jnp.repeat(steps, extent[dim] // shards_of).reshape([-1 if axis == dim else 1 for axis in range(len(extent))])
    return factor_of


def bell_draw(own_key, dims, width, limit, cuts=(), kind=jnp.bfloat16):
    factor_of = shard_levels(own_key, dims, cuts, -0.22, 0.18) if cuts else 1.0
    drawn = jax.random.normal(own_key, dims, jnp.float32) * width * factor_of
    return jnp.minimum(jnp.maximum(drawn, -limit), limit).astype(kind)


def noise_with(rng, extent, scale, reach, cuts, heavy, kind=jnp.bfloat16):
    entries = scale * jax.random.normal(rng, extent, jnp.float32)
    if cuts:
        entries = entries * shard_levels(rng, extent, cuts, -0.22, 0.18)
    return jnp.clip(with_spikes(entries, jax.random.fold_in(rng, 3), *heavy), -reach, reach).astype(kind)


def setup_inputs(seed: int = 0) -> dict:
    arg_keys = jax.random.split(jax.random.key(seed), 8)
    return {
        "features": noise_with(arg_keys[0], (ROWS, D_IN), 1.0, 6.0, ((0, 32),), (0, 1, 32, 2.75)),
        "w_first": bell_draw(arg_keys[1], (D_IN, HIDDEN_SIZE), D_IN ** -0.5, 0.125),
        "bn_gain": jnp.clip(1.0 + 0.18 * jax.random.normal(arg_keys[2], (HIDDEN_SIZE,), jnp.float32), 0.1, 1.9),
        "bn_bias": bell_draw(arg_keys[3], (HIDDEN_SIZE,), 0.5, 3.0, (), jnp.float32),
        "w_second": bell_draw(arg_keys[4], (HIDDEN_SIZE, EMBED), HIDDEN_SIZE ** -0.5, 0.125),
        "prototypes": draw_prototypes(jax.random.fold_in(arg_keys[7], 71), 0),
        "pair": draw_pair(jax.random.fold_in(arg_keys[7], 71), 0),
    }


transport_entropy_weight = 0.05
sharpness_divisor = 0.1

def unit_rows(values):
    rescaling_multiplier = lax.rsqrt(lax.optimization_barrier(jnp.sum(values * values, axis=1, keepdims=True)) + 1e-06)
    return (values * rescaling_multiplier, rescaling_multiplier)

def reference(features, w_first, bn_gain, bn_bias, w_second, prototypes, pair):
    pre = jnp.dot(features, w_first, preferred_element_type=jnp.float32)
    mean_act = lax.optimization_barrier(jnp.sum(pre, axis=0)) / ROWS
    second_moment = lax.optimization_barrier(jnp.sum(pre * pre, axis=0)) / ROWS
    inv_std = lax.rsqrt(second_moment - mean_act * mean_act + 1e-05)
    normed = (pre - mean_act) * inv_std
    shifted = normed * bn_gain + bn_bias
    hidden = jax.nn.gelu(shifted).astype(jnp.bfloat16)
    embed = jnp.dot(hidden, w_second, preferred_element_type=jnp.float32)
    unit_embed, embed_scale = unit_rows(embed)
    embed_bf = unit_embed.astype(jnp.bfloat16)
    unit_proto, proto_scale = unit_rows(prototypes.astype(jnp.float32))
    proto_bf = unit_proto.astype(jnp.bfloat16)
    block = GROUP_ROWS * min(N_BATCH, max(1, 4096 // GROUP_ROWS))
    nblocks = ROWS // block
    embed_blocks = embed_bf.reshape(nblocks, block, EMBED)

    def evaluate_similarities(sample_lowprecision):
        return lax.dot_general(sample_lowprecision, proto_bf, (((1,), (1,)), ((), ())), preferred_element_type=jnp.float32)

    def kernel_of(sample_lowprecision):
        return jnp.exp(evaluate_similarities(sample_lowprecision) / transport_entropy_weight)
    sample_normalizer = jnp.ones((nblocks, block), jnp.float32)
    per_cluster_multiplier = jnp.ones((PROTOS,), jnp.float32)
    for step in range(ITERS):

        def add_columns(total, item):
            sample_lowprecision, rescaling_multiplier = item
            return (total + jnp.dot(rescaling_multiplier, kernel_of(sample_lowprecision), precision=lax.Precision.HIGHEST), None)
        col_total = lax.scan(add_columns, jnp.zeros((PROTOS,), jnp.float32), (embed_blocks, sample_normalizer))[0]
        per_cluster_multiplier = 1.0 / col_total

        def row_pass(sample_lowprecision):
            return 1.0 / jnp.dot(kernel_of(sample_lowprecision), per_cluster_multiplier, precision=lax.Precision.HIGHEST)
        sample_normalizer = lax.map(row_pass, embed_blocks)

    def final_pass(carry, item):
        proto_acc, loss_acc = carry
        sample_lowprecision, rescaling_multiplier, mates, first = item
        centroid_similarity_matrix = evaluate_similarities(sample_lowprecision)
        cluster_allocation = jnp.exp(centroid_similarity_matrix / transport_entropy_weight) * rescaling_multiplier[:, None] * per_cluster_multiplier[None, :]
        goal_allocations = jnp.take(cluster_allocation, (mates - first).astype(jnp.int32), axis=0)
        centroid_affinities = centroid_similarity_matrix / sharpness_divisor
        exponentiated_entries = jnp.exp(centroid_affinities)
        normalizing_partition = lax.optimization_barrier(jnp.sum(exponentiated_entries, axis=1, keepdims=True))
        logp = centroid_affinities - jnp.log(normalizing_partition)
        loss_acc = loss_acc - jnp.sum(goal_allocations * logp)
        similarity_derivative = ((exponentiated_entries / normalizing_partition - goal_allocations) / sharpness_divisor).astype(jnp.bfloat16)
        d_rows = jnp.dot(similarity_derivative, proto_bf, preferred_element_type=jnp.float32)
        proto_acc = proto_acc + lax.dot_general(similarity_derivative, sample_lowprecision, (((0,), (0,)), ((), ())), preferred_element_type=jnp.float32)
        return ((proto_acc, loss_acc), d_rows)
    firsts = (jnp.arange(nblocks) * block).astype(jnp.int32)
    pair_blocks = pair.reshape(nblocks, block)
    start = (jnp.zeros((PROTOS, EMBED), jnp.float32), jnp.zeros((), jnp.float32))
    (proto_acc, loss_sum), d_unit = lax.scan(final_pass, start, (embed_blocks, sample_normalizer, pair_blocks, firsts))
    d_unit = d_unit.reshape(ROWS, EMBED)
    grad_proto = (proto_acc - unit_proto * lax.optimization_barrier(jnp.sum(unit_proto * proto_acc, axis=1, keepdims=True))) * proto_scale
    loss = loss_sum / ROWS
    d_embed = ((d_unit - unit_embed * lax.optimization_barrier(jnp.sum(unit_embed * d_unit, axis=1, keepdims=True))) * embed_scale).astype(jnp.bfloat16)
    grad_second = lax.dot_general(hidden, d_embed, (((0,), (0,)), ((), ())), preferred_element_type=jnp.float32)
    d_hidden = lax.dot_general(d_embed, w_second, (((1,), (1,)), ((), ())), preferred_element_type=jnp.float32)
    d_shift = jax.vjp(jax.nn.gelu, shifted)[1](d_hidden)[0]
    grad_gain = lax.optimization_barrier(jnp.sum(d_shift * normed, axis=0))
    grad_bias = lax.optimization_barrier(jnp.sum(d_shift, axis=0))
    d_pre = (bn_gain * inv_std * (d_shift - grad_bias / ROWS - normed * grad_gain / ROWS)).astype(jnp.bfloat16)
    grad_first = lax.dot_general(features, d_pre, (((0,), (0,)), ((), ())), preferred_element_type=jnp.float32)
    return (grad_first, grad_second, grad_gain, grad_bias, grad_proto, loss)
```

```python
import functools

import jax
import jax.numpy as jnp
from jax import lax
from jax.experimental import pallas as pl
from jax.experimental.pallas import tpu as pltpu
from jax.sharding import PartitionSpec as P

ITERS = 3
MESH = pl.DeviceIdType.MESH
F32 = jnp.float32
BF16 = jnp.bfloat16
GELU_C = 0.7978845608028654
GELU_A = 0.044715


def nn(a, b):
    return jnp.dot(a, b, preferred_element_type=F32)


def nt(a, b):
    return lax.dot_general(a, b, (((1,), (1,)), ((), ())), preferred_element_type=F32)


def step_kernel(
    nb, npr, pieces, tile_h, tile_k,
    feat, w1, gain, bias, w2, protos_t, pair,
    o_first, o_second, o_gain, o_bias, o_proto, o_loss,
    pre, hidden, feat_t, hid_t, feat_g, hid_g, dshift,
    st_p, st_b, emb_all, emb_t, pb, pscale, kern, col_x, row_x, rmat, amat, cvec,
    ep, rpm, softm, logm, lossv, dacc, d_x, pterm, pt_x, de_g, gb_p, gb_b, dp_g, rs_src, rs_x,
    rs2_src, rs2_x, stats,
    s_st_p, s_st_b, s_feat, s_hid, s_emb, s_col, s_row, s_d, s_pt, s_de, s_gb_p, s_gb_b,
    s_dp, s_rs, s_rs2,
):
    me_b = lax.axis_index("batch")
    me_p = lax.axis_index("proto")
    rows, hid_n = pre.shape
    d_in = feat.shape[1]
    block = rows * npr
    emb_n = w2.shape[1]
    cols = protos_t.shape[1]
    total = block * nb
    size = {"batch": nb, "proto": npr}
    me = {"batch": me_b, "proto": me_p}

    def peer(axis, d):
        return lax.rem(me[axis] + d, size[axis])

    def copies(axis, src, dst, sems, pick=lambda sem, k, d: sem.at[k, d]):
        out = []
        n = size[axis]
        for d in range(1, n):
            to, frm = lax.rem(me[axis] + d, n), lax.rem(me[axis] + n - d, n)
            send = pltpu.make_async_remote_copy(
                src_ref=src(to), dst_ref=dst(me[axis]), send_sem=pick(sems, 0, d),
                recv_sem=pick(sems, 1, d), device_id={axis: to}, device_id_type=MESH)
            recv = pltpu.make_async_remote_copy(
                src_ref=src(to), dst_ref=dst(frm), send_sem=pick(sems, 0, d),
                recv_sem=pick(sems, 1, d), device_id={axis: to}, device_id_type=MESH)
            out.append((send, recv))
        return out

    def start(cs):
        for send, _ in cs:
            send.start()
        return cs

    def recv(cs):
        for _, r in cs:
            r.wait_recv()

    def sent(cs):
        for s, _ in cs:
            s.wait_send()

    barrier = pltpu.get_barrier_semaphore()
    for axis in ("batch", "proto"):
        for d in range(1, size[axis]):
            pl.semaphore_signal(barrier, inc=1, device_id={axis: peer(axis, d)}, device_id_type=MESH)

    pending = []

    @pl.loop(0, hid_n // tile_h)
    def _(j):
        at = pl.ds(pl.multiple_of(j * tile_h, tile_h), tile_h)
        at2 = pl.ds(pl.multiple_of(hid_n + j * tile_h, tile_h), tile_h)
        x = nn(feat[...], w1[:, at])
        pre[:, at] = x
        st_p[me_p, :, at] = jnp.sum(x, axis=0, keepdims=True)
        st_p[me_p, :, at2] = jnp.sum(x * x, axis=0, keepdims=True)

    pl.semaphore_wait(barrier, nb + npr - 2)
    c_sp = start(copies("proto", lambda to: st_p.at[me_p], lambda f: st_p.at[f], s_st_p))
    share = d_in // (nb * npr)
    share_h = hid_n // (nb * npr)

    def transpose_to(dst, x):
        dst[...] = jnp.transpose(x.astype(F32)).astype(BF16).reshape(dst.shape)

    transpose_to(feat_t, feat[...])

    def spread(src, dst, sems, width):
        own = pl.ds(pl.multiple_of(me_p * rows, rows), rows)
        for b in range(nb):
            dst[pl.ds(b * width, width), own] = src[b, me_p]
        cs = []
        for b in range(nb):
            cs += start(copies(
                "proto", lambda to, b=b: src.at[b, to],
                lambda f, b=b: dst.at[pl.ds(b * width, width), pl.ds(pl.multiple_of(f * rows, rows), rows)],
                sems, lambda sem, k, d, b=b: sem.at[k, d, b]))
        return cs

    recv(c_sp)
    acc = st_p[0]
    for p in range(1, npr):
        acc = acc + st_p[p]
    st_b[me_b] = acc
    c_sb = start(copies("batch", lambda to: st_b.at[me_b], lambda f: st_b.at[f], s_st_b))
    pending += [c_sp, c_sb]
    c_feat = spread(feat_t, feat_g, s_feat, share)
    pending.append(c_feat)

    @pl.loop(0, cols // tile_k)
    def _(j):
        at = pl.ds(pl.multiple_of(j * tile_k, tile_k), tile_k)
        x = protos_t[:, at].astype(F32)
        sc = lax.rsqrt(jnp.sum(x * x, axis=0, keepdims=True) + 1e-06)
        pscale[:, at] = sc
        pb[:, at] = (x * sc).astype(BF16)

    recv(c_sb)
    acc = st_b[0]
    for b in range(1, nb):
        acc = acc + st_b[b]
    mean = acc[:, :hid_n] / total
    inv_std = lax.rsqrt(acc[:, hid_n:] / total - mean * mean + 1e-05)
    stats[:, :hid_n] = mean
    stats[:, hid_n:] = inv_std

    def norm_tile(at, at2):
        return (pre[:, at] - stats[:, at]) * stats[:, at2]

    dacc[0:rows, :] = jnp.zeros((rows, emb_n), F32)

    @pl.loop(0, hid_n // tile_h)
    def _(j):
        at = pl.ds(pl.multiple_of(j * tile_h, tile_h), tile_h)
        at2 = pl.ds(pl.multiple_of(hid_n + j * tile_h, tile_h), tile_h)
        x = norm_tile(at, at2) * gain[:, at] + bias[:, at]
        t = jnp.tanh(GELU_C * (x + GELU_A * (x * x * x)))
        h = (x * (0.5 * (1.0 + t))).astype(BF16)
        hidden[:, at] = h
        dacc[0:rows, :] += nn(h, w2[at, :])

    embed = dacc[0:rows, :]
    escale = lax.rsqrt(jnp.sum(embed * embed, axis=1, keepdims=True) + 1e-06)
    unit = embed * escale
    mine = pl.ds(pl.multiple_of(me_p * rows, rows), rows)
    emb_all[mine, :] = unit.astype(BF16)
    c_emb = start(copies(
        "proto", lambda to: emb_all.at[mine],
        lambda f: emb_all.at[pl.ds(pl.multiple_of(f * rows, rows), rows)], s_emb))
    pending.append(c_emb)
    transpose_to(hid_t, hidden[...])
    c_hid = spread(hid_t, hid_g, s_hid, share_h)
    pending.append(c_hid)
    hits = lax.broadcasted_iota(jnp.int32, (block, block), 0) == (pair[...] - me_b * block)
    recv(c_emb)

    amat[...] = jnp.zeros_like(amat)

    @pl.loop(0, cols // tile_k)
    def _(j):
        at = pl.ds(pl.multiple_of(j * tile_k, tile_k), tile_k)
        e = jnp.exp(10.0 * nn(emb_all[...], pb[:, at]))
        part = e[:, 0:128]
        for q in range(1, tile_k // 128):
            part = part + e[:, q * 128:(q + 1) * 128]
        amat[...] += part
        k = e * e
        kern[:, at] = k
        col_x[0, me_b, :, at] = jnp.sum(k, axis=0, keepdims=True)

    soft_row = jnp.sum(jnp.transpose(amat[...]), axis=0, keepdims=True)

    lanes = 128
    chunk = 64
    for it in range(ITERS):
        if it > 0:
            @pl.loop(0, cols // lanes)
            def _(j):
                at = pl.ds(pl.multiple_of(j * lanes, lanes), lanes)
                col_x[it, me_b, :, at] = jnp.sum(kern[:, at] * rmat[...], axis=0, keepdims=True)
        c = start(copies("batch", lambda to: col_x.at[it, me_b], lambda f: col_x.at[it, f],
                         s_col, lambda sem, k, d: sem.at[it, k, d]))
        pending.append(c)
        recv(c)
        acc = col_x[it, 0]
        for b in range(1, nb):
            acc = acc + col_x[it, b]
        cvec[...] = 1.0 / acc

        @pl.loop(0, block // chunk)
        def _(i):
            at = pl.ds(pl.multiple_of(i * chunk, chunk), chunk)
            a = kern[at, 0:lanes] * cvec[:, 0:lanes]
            for q in range(1, cols // lanes):
                a = a + kern[at, q * lanes:(q + 1) * lanes] * cvec[:, q * lanes:(q + 1) * lanes]
            amat[at, :] = a

        row_x[it, me_p, :, 0:block] = jnp.sum(jnp.transpose(amat[...]), axis=0, keepdims=True)
        row_x[it, me_p, :, block:] = soft_row
        c = start(copies("proto", lambda to: row_x.at[it, me_p], lambda f: row_x.at[it, f],
                         s_row, lambda sem, k, d: sem.at[it, k, d]))
        pending.append(c)
        recv(c)
        acc = row_x[it, 0]
        for p in range(1, npr):
            acc = acc + row_x[it, p]
        r_row = 1.0 / acc[:, :block]
        if it < ITERS - 1:
            rmat[...] = jnp.transpose(jnp.broadcast_to(r_row, (lanes, block)))
        else:
            soft = jnp.transpose(jnp.broadcast_to(acc[:, block:], (lanes, block)))
            softm[...] = 10.0 / soft
            logm[...] = jnp.log(soft)
            rp = jnp.sum(jnp.where(hits, r_row, 0.0), axis=1, keepdims=True)
            rpm[...] = jnp.broadcast_to(rp, (block, lanes))

    ep[...] = nn(jnp.where(hits, 1.0, 0.0).astype(BF16), emb_all[...]).astype(BF16)
    emb_t[...] = jnp.transpose(emb_all[...].astype(F32)).astype(BF16)
    dacc[...] = jnp.zeros_like(dacc)
    lossv[...] = jnp.zeros_like(lossv)
    reps = tile_k // lanes

    def wide(ref):
        return jnp.concatenate([ref[...]] * reps, axis=1)

    @pl.loop(0, cols // tile_k)
    def _(j):
        at = pl.ds(pl.multiple_of(j * tile_k, tile_k), tile_k)
        s = 10.0 * nn(emb_all[...], pb[:, at])
        goal = jnp.exp(20.0 * nn(ep[...], pb[:, at])) * wide(rpm) * cvec[:, at]
        lossv[...] -= jnp.sum(goal * (s - wide(logm)), axis=0, keepdims=True)
        g = (jnp.exp(s) * wide(softm) - 10.0 * goal).astype(BF16)
        dacc[...] += nt(g, pb[:, at])
        acc = nn(emb_t[...], g)
        sc = pscale[:, at]
        up = protos_t[:, at].astype(F32) * sc
        term = (acc - up * jnp.sum(up * acc, axis=0, keepdims=True)) * sc
        pterm[:, at] = term.astype(BF16)

    c_d = start(copies(
        "proto", lambda to: dacc.at[pl.ds(pl.multiple_of(to * rows, rows), rows)],
        lambda f: d_x.at[f], s_d))
    emb_share = emb_n // nb
    c_pt = start(copies(
        "batch", lambda to: pterm.at[pl.ds(pl.multiple_of(to * emb_share, emb_share), emb_share)],
        lambda f: pt_x.at[f], s_pt))
    pending += [c_d, c_pt]
    d_x[me_p] = dacc[mine, :]
    recv(c_d)
    d_unit = d_x[0]
    for p in range(1, npr):
        d_unit = d_unit + d_x[p]
    d_embed = ((d_unit - unit * jnp.sum(unit * d_unit, axis=1, keepdims=True)) * escale).astype(BF16)
    de_g[mine, :] = d_embed
    c_de = start(copies(
        "proto", lambda to: de_g.at[mine],
        lambda f: de_g.at[pl.ds(pl.multiple_of(f * rows, rows), rows)], s_de))
    pending.append(c_de)

    @pl.loop(0, hid_n // tile_h)
    def _(j):
        at = pl.ds(pl.multiple_of(j * tile_h, tile_h), tile_h)
        at2 = pl.ds(pl.multiple_of(hid_n + j * tile_h, tile_h), tile_h)
        dh = nt(de_g[mine, :], w2[at, :])
        nrm = norm_tile(at, at2)
        x = nrm * gain[:, at] + bias[:, at]
        t = jnp.tanh(GELU_C * (x + GELU_A * (x * x * x)))
        slope = 0.5 * (1.0 + t) + 0.5 * x * (1.0 - t * t) * (GELU_C * (1.0 + 3.0 * GELU_A * (x * x)))
        ds = slope * dh
        dshift[:, at] = ds
        gb_p[me_p, :, at] = jnp.sum(ds * nrm, axis=0, keepdims=True)
        gb_p[me_p, :, at2] = jnp.sum(ds, axis=0, keepdims=True)

    gb_p[me_p, :, 2 * hid_n:] = jnp.broadcast_to(jnp.sum(lossv[...], axis=1, keepdims=True), (1, lanes))
    c_gp = start(copies("proto", lambda to: gb_p.at[me_p], lambda f: gb_p.at[f], s_gb_p))
    recv(c_gp)
    acc = gb_p[0]
    for p in range(1, npr):
        acc = acc + gb_p[p]
    gb_b[me_b] = acc
    c_gb = start(copies("batch", lambda to: gb_b.at[me_b], lambda f: gb_b.at[f], s_gb_b))
    pending += [c_gp, c_gb]

    recv(c_hid)
    recv(c_de)
    rs2_src[...] = nn(hid_g[...], de_g[...]).astype(BF16)
    c_rs2 = start(copies(
        "batch", lambda to: rs2_src.at[pl.ds(pl.multiple_of(to * share_h, share_h), share_h)],
        lambda f: rs2_x.at[f], s_rs2))
    pending.append(c_rs2)
    rs2_x[me_b] = rs2_src[pl.ds(pl.multiple_of(me_b * share_h, share_h), share_h), :]
    recv(c_feat)

    recv(c_gb)
    acc = gb_b[0]
    for b in range(1, nb):
        acc = acc + gb_b[b]
    o_gain[...] = acc[:, :hid_n]
    o_bias[...] = acc[:, hid_n:2 * hid_n]
    o_loss[...] = acc[:, 2 * hid_n:] / total

    width = hid_n // pieces
    c_dp = []
    for q in range(pieces):
        at = slice(q * width, (q + 1) * width)
        at2 = slice(hid_n + q * width, hid_n + (q + 1) * width)
        nrm = norm_tile(at, at2)
        dp = gain[:, at] * stats[:, at2] * (
            dshift[:, at] - o_bias[:, at] / total - nrm * (o_gain[:, at] / total))
        dp_g[q, mine, :] = dp.astype(BF16)
        c_dp.append(start(copies(
            "proto", lambda to, q=q: dp_g.at[q, mine],
            lambda f, q=q: dp_g.at[q, pl.ds(pl.multiple_of(f * rows, rows), rows)],
            s_dp, lambda sem, k, d, q=q: sem.at[k, d, q])))
    c_rs = []
    for q in range(pieces):
        recv(c_dp[q])
        rs_src[q] = nn(feat_g[...], dp_g[q]).astype(BF16)
        c_rs.append(start(copies(
            "batch", lambda to, q=q: rs_src.at[q, pl.ds(pl.multiple_of(to * share, share), share)],
            lambda f, q=q: rs_x.at[f, q],
            s_rs, lambda sem, k, d, q=q: sem.at[k, d, q])))
        rs_x[me_b, q] = rs_src[q, pl.ds(pl.multiple_of(me_b * share, share), share), :]
    pending += c_dp + c_rs

    pt_x[me_b] = pterm[pl.ds(pl.multiple_of(me_b * emb_share, emb_share), emb_share), :]
    recv(c_pt)

    @pl.loop(0, cols // tile_k)
    def _(j):
        at = pl.ds(pl.multiple_of(j * tile_k, tile_k), tile_k)
        acc = pt_x[0, :, at].astype(F32)
        for b in range(1, nb):
            acc = acc + pt_x[b, :, at].astype(F32)
        o_proto[:, at] = acc

    recv(c_rs2)
    acc = rs2_x[0].astype(F32)
    for b in range(1, nb):
        acc = acc + rs2_x[b].astype(F32)
    o_second[...] = acc
    for q in range(pieces):
        recv(c_rs[q])
        acc = rs_x[0, q].astype(F32)
        for b in range(1, nb):
            acc = acc + rs_x[b, q].astype(F32)
        o_first[:, q * width:(q + 1) * width] = acc
    for cs in pending:
        sent(cs)


def local(features, w_first, bn_gain, bn_bias, w_second, prototypes, pair):
    nb = lax.axis_size("batch")
    npr = lax.axis_size("proto")
    rows, d_in = features.shape
    hid_n, emb_n = w_second.shape
    cols = prototypes.shape[0]
    block = rows * npr
    share, share_h, emb_share = d_in // (nb * npr), hid_n // (nb * npr), emb_n // nb
    pieces = 4
    width = hid_n // pieces
    tile_h = min(256, hid_n)
    tile_k = 256
    dma = pltpu.SemaphoreType.DMA
    V = pltpu.VMEM
    scratch = [
        V((rows, hid_n), F32), V((rows, hid_n), BF16),
        V((nb, npr, share, rows), BF16), V((nb, npr, share_h, rows), BF16),
        V((nb * share, block), BF16), V((nb * share_h, block), BF16),
        V((rows, hid_n), F32),
        V((npr, 1, 2 * hid_n), F32), V((nb, 1, 2 * hid_n), F32),
        V((block, emb_n), BF16), V((emb_n, block), BF16),
        V((emb_n, cols), BF16), V((1, cols), F32), V((block, cols), F32),
        V((ITERS, nb, 1, cols), F32), V((ITERS, npr, 1, 2 * block), F32),
        V((block, 128), F32), V((block, 128), F32), V((1, cols), F32),
        V((block, emb_n), BF16), V((block, 128), F32), V((block, 128), F32), V((block, 128), F32),
        V((1, tile_k), F32), V((block, emb_n), F32), V((npr, rows, emb_n), F32),
        V((emb_n, cols), BF16), V((nb, emb_share, cols), BF16), V((block, emb_n), BF16),
        V((npr, 1, 2 * hid_n + 128), F32), V((nb, 1, 2 * hid_n + 128), F32),
        V((pieces, block, width), BF16),
        V((pieces, nb * share, width), BF16), V((nb, pieces, share, width), BF16),
        V((nb * share_h, emb_n), BF16), V((nb, share_h, emb_n), BF16),
        V((1, 2 * hid_n), F32),
        dma((2, npr)), dma((2, nb)), dma((2, npr, nb)), dma((2, npr, nb)), dma((2, npr)),
        dma((ITERS, 2, nb)), dma((ITERS, 2, npr)), dma((2, npr)), dma((2, nb)), dma((2, npr)),
        dma((2, npr)), dma((2, nb)), dma((2, npr, pieces)), dma((2, nb, pieces)), dma((2, nb)),
    ]
    vm = pl.BlockSpec(memory_space=pltpu.VMEM)
    sds = jax.ShapeDtypeStruct
    first, second, gain, bias, proto_t, loss = pl.pallas_call(
        functools.partial(step_kernel, nb, npr, pieces, tile_h, tile_k),
        out_shape=[
            sds((share, hid_n), F32), sds((share_h, emb_n), F32), sds((1, hid_n), F32),
            sds((1, hid_n), F32), sds((emb_share, cols), F32), sds((1, 128), F32),
        ],
        in_specs=[vm] * 7,
        out_specs=[vm] * 6,
        scratch_shapes=scratch,
        compiler_params=pltpu.CompilerParams(
            collective_id=0, has_side_effects=True, vmem_limit_bytes=60 * 1024 * 1024),
    )(features, w_first, bn_gain[None], bn_bias[None], w_second, prototypes.T, pair[None])
    return first, second, gain[0], bias[0], proto_t.T, loss[0, 0]


def solution(mesh):
    return jax.shard_map(
        local,
        mesh=mesh,
        in_specs=(P(("batch", "proto"), None), P(), P(), P(), P(), P("proto", None), P("batch")),
        out_specs=(
            P(("batch", "proto"), None),
            P(("batch", "proto"), None),
            P(),
            P(),
            P("proto", "batch"),
            P(),
        ),
        check_vma=False,
    )
```

```python
import functools

import jax
import jax.numpy as jnp
from jax import lax
from jax.experimental import pallas as pl
from jax.experimental.pallas import tpu as pltpu
from jax.sharding import PartitionSpec as P

ITERS = 3
MESH = pl.DeviceIdType.MESH
F32 = jnp.float32
BF16 = jnp.bfloat16
GELU_C = 0.7978845608028654
GELU_A = 0.044715


def nn(a, b):
    return jnp.dot(a, b, preferred_element_type=F32)


def nt(a, b):
    return lax.dot_general(a, b, (((1,), (1,)), ((), ())), preferred_element_type=F32)


def inner_sizes(nb, npr):
    inner = 2 ** ((nb.bit_length() - 1) // 2)
    return inner if nb % inner == 0 else 1, 2 if npr % 2 == 0 else 1


def step_kernel(
    nb, npr, pieces, tile_h, tile_k,
    feat, w1, gain, bias, w2, protos, pair,
    o_first, o_second, o_gain, o_bias, o_proto, o_loss,
    pre, hidden, feat_t, hid_t, feat_g, hid_g, dshift,
    st_p, st_b, emb_all, emb_t, pb, pscale, kern, col_x, row_x, rmat, amat, cvec,
    ep, rpm, softm, logm, lossv, dacc, d_x, pterm, pt_x, de_g, gb_p, gb_b, dp_g, rs_src, rs_x,
    rs2_src, rs2_x, stats, protos_t, pt_y, pt_x2, rs_y, rs_x2,
    s_st_p, s_st_b, s_feat, s_hid, s_emb, s_col, s_row, s_d, s_pt, s_de, s_gb_p, s_gb_b,
    s_dph, s_dpl, s_dpf, s_rs, s_rs2, s_pt2, s_rsb,
):
    me_b = lax.axis_index("batch")
    me_p = lax.axis_index("proto")
    rows, hid_n = pre.shape
    d_in = feat.shape[1]
    block = rows * npr
    emb_n = w2.shape[1]
    cols = protos.shape[0]
    total = block * nb
    b_lo, p_lo = inner_sizes(nb, npr)
    b_hi, p_hi = nb // b_lo, npr // p_lo
    bh, bl, ph, pq = me_b // b_lo, me_b % b_lo, me_p // p_lo, me_p % p_lo
    size = {"batch": nb, "proto": npr, "b_lo": b_lo, "b_hi": b_hi, "p_lo": p_lo, "p_hi": p_hi}
    me = {"batch": me_b, "proto": me_p, "b_lo": bl, "b_hi": bh, "p_lo": pq, "p_hi": ph}
    place = {
        "batch": lambda i: {"batch": i}, "proto": lambda i: {"proto": i},
        "b_lo": lambda i: {"batch": bh * b_lo + i}, "b_hi": lambda i: {"batch": i * b_lo + bl},
        "p_lo": lambda i: {"proto": ph * p_lo + i}, "p_hi": lambda i: {"proto": i * p_lo + pq},
    }

    def peer(axis, d):
        return lax.rem(me[axis] + d, size[axis])

    def copies(axis, src, dst, sems, pick=lambda sem, k, d: sem.at[k, d]):
        out = []
        n = size[axis]
        for d in range(1, n):
            to, frm = lax.rem(me[axis] + d, n), lax.rem(me[axis] + n - d, n)
            send = pltpu.make_async_remote_copy(
                src_ref=src(to), dst_ref=dst(me[axis]), send_sem=pick(sems, 0, d),
                recv_sem=pick(sems, 1, d), device_id=place[axis](to), device_id_type=MESH)
            recv = pltpu.make_async_remote_copy(
                src_ref=src(to), dst_ref=dst(frm), send_sem=pick(sems, 0, d),
                recv_sem=pick(sems, 1, d), device_id=place[axis](to), device_id_type=MESH)
            out.append((send, recv))
        return out

    def start(cs):
        for send, _ in cs:
            send.start()
        return cs

    def recv(cs):
        for _, r in cs:
            r.wait_recv()

    def sent(cs):
        for s, _ in cs:
            s.wait_send()

    barrier = pltpu.get_barrier_semaphore()
    for axis in ("batch", "proto"):
        for d in range(1, size[axis]):
            pl.semaphore_signal(barrier, inc=1, device_id={axis: peer(axis, d)}, device_id_type=MESH)

    pending = []

    @pl.loop(0, hid_n // tile_h)
    def _(j):
        at = pl.ds(pl.multiple_of(j * tile_h, tile_h), tile_h)
        at2 = pl.ds(pl.multiple_of(hid_n + j * tile_h, tile_h), tile_h)
        x = nn(feat[...], w1[:, at])
        pre[:, at] = x
        st_p[me_p, :, at] = jnp.sum(x, axis=0, keepdims=True)
        st_p[me_p, :, at2] = jnp.sum(x * x, axis=0, keepdims=True)

    pl.semaphore_wait(barrier, nb + npr - 2)
    c_sp = start(copies("proto", lambda to: st_p.at[me_p], lambda f: st_p.at[f], s_st_p))
    share = d_in // (nb * npr)
    share_h = hid_n // (nb * npr)

    def transpose_to(dst, x):
        dst[...] = jnp.transpose(x.astype(F32)).astype(BF16).reshape(dst.shape)

    transpose_to(feat_t, feat[...])

    def spread(src, dst, sems, width):
        own = pl.ds(pl.multiple_of(me_p * rows, rows), rows)
        for b in range(nb):
            dst[pl.ds(b * width, width), own] = src[b, me_p]
        cs = []
        for b in range(nb):
            cs += start(copies(
                "proto", lambda to, b=b: src.at[b, to],
                lambda f, b=b: dst.at[pl.ds(b * width, width), pl.ds(pl.multiple_of(f * rows, rows), rows)],
                sems, lambda sem, k, d, b=b: sem.at[k, d, b]))
        return cs

    recv(c_sp)
    acc = st_p[0]
    for p in range(1, npr):
        acc = acc + st_p[p]
    st_b[me_b] = acc
    c_sb = start(copies("batch", lambda to: st_b.at[me_b], lambda f: st_b.at[f], s_st_b))
    pending += [c_sp, c_sb]
    c_feat = spread(feat_t, feat_g, s_feat, share)
    pending.append(c_feat)

    @pl.loop(0, cols // tile_k)
    def _(j):
        at = pl.ds(pl.multiple_of(j * tile_k, tile_k), tile_k)
        x = jnp.transpose(protos[at, :].astype(F32))
        protos_t[:, at] = x.astype(BF16)
        sc = lax.rsqrt(jnp.sum(x * x, axis=0, keepdims=True) + 1e-06)
        pscale[:, at] = sc
        pb[:, at] = (x * sc).astype(BF16)

    recv(c_sb)
    acc = st_b[0]
    for b in range(1, nb):
        acc = acc + st_b[b]
    mean = acc[:, :hid_n] / total
    inv_std = lax.rsqrt(acc[:, hid_n:] / total - mean * mean + 1e-05)
    stats[:, :hid_n] = mean
    stats[:, hid_n:] = inv_std

    def norm_tile(at, at2):
        return (pre[:, at] - stats[:, at]) * stats[:, at2]

    dacc[0:rows, :] = jnp.zeros((rows, emb_n), F32)

    @pl.loop(0, hid_n // tile_h)
    def _(j):
        at = pl.ds(pl.multiple_of(j * tile_h, tile_h), tile_h)
        at2 = pl.ds(pl.multiple_of(hid_n + j * tile_h, tile_h), tile_h)
        x = norm_tile(at, at2) * gain[:, at] + bias[:, at]
        t = jnp.tanh(GELU_C * (x + GELU_A * (x * x * x)))
        h = (x * (0.5 * (1.0 + t))).astype(BF16)
        hidden[:, at] = h
        dacc[0:rows, :] += nn(h, w2[at, :])

    embed = dacc[0:rows, :]
    escale = lax.rsqrt(jnp.sum(embed * embed, axis=1, keepdims=True) + 1e-06)
    unit = embed * escale
    mine = pl.ds(pl.multiple_of(me_p * rows, rows), rows)
    emb_all[mine, :] = unit.astype(BF16)
    c_emb = start(copies(
        "proto", lambda to: emb_all.at[mine],
        lambda f: emb_all.at[pl.ds(pl.multiple_of(f * rows, rows), rows)], s_emb))
    pending.append(c_emb)
    transpose_to(hid_t, hidden[...])
    c_hid = spread(hid_t, hid_g, s_hid, share_h)
    pending.append(c_hid)
    hits = lax.broadcasted_iota(jnp.int32, (block, block), 0) == (pair[...] - me_b * block)
    recv(c_emb)

    amat[...] = jnp.zeros_like(amat)

    @pl.loop(0, cols // tile_k)
    def _(j):
        at = pl.ds(pl.multiple_of(j * tile_k, tile_k), tile_k)
        e = jnp.exp(10.0 * nn(emb_all[...], pb[:, at]))
        part = e[:, 0:128]
        for q in range(1, tile_k // 128):
            part = part + e[:, q * 128:(q + 1) * 128]
        amat[...] += part
        k = e * e
        kern[:, at] = k
        col_x[0, me_b, :, at] = jnp.sum(k, axis=0, keepdims=True)

    soft_row = jnp.sum(jnp.transpose(amat[...]), axis=0, keepdims=True)

    lanes = 128
    chunk = 64
    for it in range(ITERS):
        if it > 0:
            @pl.loop(0, cols // lanes)
            def _(j):
                at = pl.ds(pl.multiple_of(j * lanes, lanes), lanes)
                col_x[it, me_b, :, at] = jnp.sum(kern[:, at] * rmat[...], axis=0, keepdims=True)
        c = start(copies("batch", lambda to: col_x.at[it, me_b], lambda f: col_x.at[it, f],
                         s_col, lambda sem, k, d: sem.at[it, k, d]))
        pending.append(c)
        recv(c)
        acc = col_x[it, 0]
        for b in range(1, nb):
            acc = acc + col_x[it, b]
        cvec[...] = 1.0 / acc

        @pl.loop(0, block // chunk)
        def _(i):
            at = pl.ds(pl.multiple_of(i * chunk, chunk), chunk)
            a = kern[at, 0:lanes] * cvec[:, 0:lanes]
            for q in range(1, cols // lanes):
                a = a + kern[at, q * lanes:(q + 1) * lanes] * cvec[:, q * lanes:(q + 1) * lanes]
            amat[at, :] = a

        row_x[it, me_p, :, 0:block] = jnp.sum(jnp.transpose(amat[...]), axis=0, keepdims=True)
        row_x[it, me_p, :, block:] = soft_row
        c = start(copies("proto", lambda to: row_x.at[it, me_p], lambda f: row_x.at[it, f],
                         s_row, lambda sem, k, d: sem.at[it, k, d]))
        pending.append(c)
        recv(c)
        acc = row_x[it, 0]
        for p in range(1, npr):
            acc = acc + row_x[it, p]
        r_row = 1.0 / acc[:, :block]
        if it < ITERS - 1:
            rmat[...] = jnp.transpose(jnp.broadcast_to(r_row, (lanes, block)))
        else:
            soft = jnp.transpose(jnp.broadcast_to(acc[:, block:], (lanes, block)))
            softm[...] = 10.0 / soft
            logm[...] = jnp.log(soft)
            rp = jnp.sum(jnp.where(hits, r_row, 0.0), axis=1, keepdims=True)
            rpm[...] = jnp.broadcast_to(rp, (block, lanes))

    ep[...] = nn(jnp.where(hits, 1.0, 0.0).astype(BF16), emb_all[...]).astype(BF16)
    emb_t[...] = jnp.transpose(emb_all[...].astype(F32)).astype(BF16)
    dacc[...] = jnp.zeros_like(dacc)
    lossv[...] = jnp.zeros_like(lossv)
    reps = tile_k // lanes

    def wide(ref):
        return jnp.concatenate([ref[...]] * reps, axis=1)

    emb_share = emb_n // nb
    group = cols // pieces

    def tile_step(g, j):
        at = pl.ds(pl.multiple_of(g * group + j * tile_k, tile_k), tile_k)
        at_g = pl.ds(pl.multiple_of(j * tile_k, tile_k), tile_k)
        s = 10.0 * nn(emb_all[...], pb[:, at])
        goal = jnp.exp(20.0 * nn(ep[...], pb[:, at])) * wide(rpm) * cvec[:, at]
        lossv[...] -= jnp.sum(goal * (s - wide(logm)), axis=0, keepdims=True)
        gs = (jnp.exp(s) * wide(softm) - 10.0 * goal).astype(BF16)
        dacc[...] += nt(gs, pb[:, at])
        acc = nn(emb_t[...], gs)
        sc = pscale[:, at]
        up = protos_t[:, at].astype(F32) * sc
        term = (acc - up * jnp.sum(up * acc, axis=0, keepdims=True)) * sc
        pterm[g, :, :, :, at_g] = term.astype(BF16).reshape(b_hi, b_lo, emb_share, tile_k)

    c_pt = []
    for g in range(pieces):
        @pl.loop(0, group // tile_k)
        def _(j):
            tile_step(g, j)

        c_pt.append(start(copies(
            "b_lo", lambda to: pterm.at[g, :, to], lambda f: pt_x.at[g, f],
            s_pt, lambda sem, k, d: sem.at[k, d, g])))

    c_d = start(copies(
        "proto", lambda to: dacc.at[pl.ds(pl.multiple_of(to * rows, rows), rows)],
        lambda f: d_x.at[f], s_d))
    pending += [c_d] + c_pt
    c_pt2 = []

    def forward_pt(g):
        pt_x[g, bl] = pterm[g, :, bl]
        recv(c_pt[g])
        for h in range(b_hi):
            acc = pt_x[g, 0, h].astype(F32)
            for l in range(1, b_lo):
                acc = acc + pt_x[g, l, h].astype(F32)
            pt_y[g, h] = acc.astype(BF16)
        c_pt2.append(start(copies(
            "b_hi", lambda to: pt_y.at[g, to], lambda f: pt_x2.at[g, f],
            s_pt2, lambda sem, k, d: sem.at[k, d, g])))

    half = pieces // 2
    for g in range(half):
        forward_pt(g)
    d_x[me_p] = dacc[mine, :]
    recv(c_d)
    d_unit = d_x[0]
    for p in range(1, npr):
        d_unit = d_unit + d_x[p]
    d_embed = ((d_unit - unit * jnp.sum(unit * d_unit, axis=1, keepdims=True)) * escale).astype(BF16)
    de_g[mine, :] = d_embed
    c_de = start(copies(
        "proto", lambda to: de_g.at[mine],
        lambda f: de_g.at[pl.ds(pl.multiple_of(f * rows, rows), rows)], s_de))
    pending.append(c_de)

    @pl.loop(0, hid_n // tile_h)
    def _(j):
        at = pl.ds(pl.multiple_of(j * tile_h, tile_h), tile_h)
        at2 = pl.ds(pl.multiple_of(hid_n + j * tile_h, tile_h), tile_h)
        dh = nt(de_g[mine, :], w2[at, :])
        nrm = norm_tile(at, at2)
        x = nrm * gain[:, at] + bias[:, at]
        t = jnp.tanh(GELU_C * (x + GELU_A * (x * x * x)))
        slope = 0.5 * (1.0 + t) + 0.5 * x * (1.0 - t * t) * (GELU_C * (1.0 + 3.0 * GELU_A * (x * x)))
        ds = slope * dh
        dshift[:, at] = ds
        gb_p[me_p, :, at] = jnp.sum(ds * nrm, axis=0, keepdims=True)
        gb_p[me_p, :, at2] = jnp.sum(ds, axis=0, keepdims=True)

    gb_p[me_p, :, 2 * hid_n:] = jnp.broadcast_to(jnp.sum(lossv[...], axis=1, keepdims=True), (1, lanes))
    c_gp = start(copies("proto", lambda to: gb_p.at[me_p], lambda f: gb_p.at[f], s_gb_p))
    for g in range(half, pieces):
        forward_pt(g)
    pending += c_pt2
    recv(c_gp)
    acc = gb_p[0]
    for p in range(1, npr):
        acc = acc + gb_p[p]
    gb_b[me_b] = acc
    c_gb = start(copies("batch", lambda to: gb_b.at[me_b], lambda f: gb_b.at[f], s_gb_b))
    pending += [c_gp, c_gb]

    recv(c_hid)
    recv(c_de)
    rs2_src[...] = nn(hid_g[...], de_g[...]).astype(BF16)
    c_rs2 = start(copies(
        "batch", lambda to: rs2_src.at[pl.ds(pl.multiple_of(to * share_h, share_h), share_h)],
        lambda f: rs2_x.at[f], s_rs2))
    pending.append(c_rs2)
    rs2_x[me_b] = rs2_src[pl.ds(pl.multiple_of(me_b * share_h, share_h), share_h), :]
    recv(c_feat)

    recv(c_gb)
    acc = gb_b[0]
    for b in range(1, nb):
        acc = acc + gb_b[b]
    o_gain[...] = acc[:, :hid_n]
    o_bias[...] = acc[:, hid_n:2 * hid_n]
    o_loss[...] = acc[:, 2 * hid_n:] / total

    width = hid_n // pieces

    def rows_of(q, p):
        return dp_g.at[q, pl.ds(pl.multiple_of(p * rows, rows), rows)]

    c_far, c_near = [], []
    for q in range(pieces):
        at = slice(q * width, (q + 1) * width)
        at2 = slice(hid_n + q * width, hid_n + (q + 1) * width)
        nrm = norm_tile(at, at2)
        dp = gain[:, at] * stats[:, at2] * (
            dshift[:, at] - o_bias[:, at] / total - nrm * (o_gain[:, at] / total))
        dp_g[q, mine, :] = dp.astype(BF16)
        c_far.append(start(copies(
            "p_hi", lambda to: rows_of(q, me_p), lambda f: rows_of(q, f * p_lo + pq),
            s_dph, lambda sem, k, d: sem.at[k, d, q])))
        c_near.append(start(copies(
            "p_lo", lambda to: rows_of(q, me_p), lambda f: rows_of(q, ph * p_lo + f),
            s_dpl, lambda sem, k, d: sem.at[k, d, q])))

    def pass_on(q):
        out = []
        for e in range(1, p_hi):
            recv(c_far[q][e - 1:e])
            frm = lax.rem(ph + p_hi - e, p_hi)
            out += start(copies(
                "p_lo", lambda to: rows_of(q, frm * p_lo + pq), lambda f: rows_of(q, frm * p_lo + f),
                s_dpf, lambda sem, k, d: sem.at[k, d, e, q]))
        return out

    c_rs, c_rsb = [], []

    def forward_rs(q):
        rs_x[q, bl] = rs_src[q, :, bl]
        recv(c_rs[q])
        for h in range(b_hi):
            acc = rs_x[q, 0, h].astype(F32)
            for l in range(1, b_lo):
                acc = acc + rs_x[q, l, h].astype(F32)
            rs_y[q, h] = acc.astype(BF16)
        c_rsb.append(start(copies(
            "b_hi", lambda to: rs_y.at[q, to], lambda f: rs_x2.at[q, f],
            s_rsb, lambda sem, k, d: sem.at[k, d, q])))

    c_fwd = [pass_on(0)]
    for q in range(pieces):
        recv(c_near[q])
        recv(c_fwd[q])
        rs_src[q] = nn(feat_g[...], dp_g[q]).astype(BF16).reshape(b_hi, b_lo, share, width)
        c_rs.append(start(copies(
            "b_lo", lambda to: rs_src.at[q, :, to], lambda f: rs_x.at[q, f],
            s_rs, lambda sem, k, d: sem.at[k, d, q])))
        if q + 1 < pieces:
            c_fwd.append(pass_on(q + 1))
        if q > 0:
            forward_rs(q - 1)
    forward_rs(pieces - 1)
    pending += c_far + c_near + c_fwd + c_rs + c_rsb

    for g in range(pieces):
        pt_x2[g, bh] = pt_y[g, bh]
        recv(c_pt2[g])
        acc = pt_x2[g, 0].astype(F32)
        for h in range(1, b_hi):
            acc = acc + pt_x2[g, h].astype(F32)
        o_proto[:, g * group:(g + 1) * group] = acc

    recv(c_rs2)
    acc = rs2_x[0].astype(F32)
    for b in range(1, nb):
        acc = acc + rs2_x[b].astype(F32)
    o_second[...] = acc
    for q in range(pieces):
        rs_x2[q, bh] = rs_y[q, bh]
        recv(c_rsb[q])
        acc = rs_x2[q, 0].astype(F32)
        for h in range(1, b_hi):
            acc = acc + rs_x2[q, h].astype(F32)
        o_first[:, q * width:(q + 1) * width] = acc
    for cs in pending:
        sent(cs)


def local(features, w_first, bn_gain, bn_bias, w_second, prototypes, pair):
    nb = lax.axis_size("batch")
    npr = lax.axis_size("proto")
    rows, d_in = features.shape
    hid_n, emb_n = w_second.shape
    cols = prototypes.shape[0]
    block = rows * npr
    share, share_h, emb_share = d_in // (nb * npr), hid_n // (nb * npr), emb_n // nb
    pieces = 4
    width, group = hid_n // pieces, cols // pieces
    b_lo, p_lo = inner_sizes(nb, npr)
    b_hi, p_hi = nb // b_lo, npr // p_lo
    tile_h = min(512, hid_n)
    tile_k = 256
    dma = pltpu.SemaphoreType.DMA
    V = pltpu.VMEM
    scratch = [
        V((rows, hid_n), F32), V((rows, hid_n), BF16),
        V((nb, npr, share, rows), BF16), V((nb, npr, share_h, rows), BF16),
        V((nb * share, block), BF16), V((nb * share_h, block), BF16),
        V((rows, hid_n), F32),
        V((npr, 1, 2 * hid_n), F32), V((nb, 1, 2 * hid_n), F32),
        V((block, emb_n), BF16), V((emb_n, block), BF16),
        V((emb_n, cols), BF16), V((1, cols), F32), V((block, cols), F32),
        V((ITERS, nb, 1, cols), F32), V((ITERS, npr, 1, 2 * block), F32),
        V((block, 128), F32), V((block, 128), F32), V((1, cols), F32),
        V((block, emb_n), BF16), V((block, 128), F32), V((block, 128), F32), V((block, 128), F32),
        V((1, tile_k), F32), V((block, emb_n), F32), V((npr, rows, emb_n), F32),
        V((pieces, b_hi, b_lo, emb_share, group), BF16), V((pieces, b_lo, b_hi, emb_share, group), BF16), V((block, emb_n), BF16),
        V((npr, 1, 2 * hid_n + 128), F32), V((nb, 1, 2 * hid_n + 128), F32),
        V((pieces, block, width), BF16),
        V((pieces, b_hi, b_lo, share, width), BF16), V((pieces, b_lo, b_hi, share, width), BF16),
        V((nb * share_h, emb_n), BF16), V((nb, share_h, emb_n), BF16),
        V((1, 2 * hid_n), F32), V((emb_n, cols), BF16),
        V((pieces, b_hi, emb_share, group), BF16), V((pieces, b_hi, emb_share, group), BF16),
        V((pieces, b_hi, share, width), BF16), V((pieces, b_hi, share, width), BF16),
        dma((2, npr)), dma((2, nb)), dma((2, npr, nb)), dma((2, npr, nb)), dma((2, npr)),
        dma((ITERS, 2, nb)), dma((ITERS, 2, npr)), dma((2, npr)), dma((2, b_lo, pieces)), dma((2, npr)),
        dma((2, npr)), dma((2, nb)), dma((2, p_hi, pieces)), dma((2, p_lo, pieces)),
        dma((2, p_lo, p_hi, pieces)), dma((2, b_lo, pieces)), dma((2, nb)),
        dma((2, b_hi, pieces)), dma((2, b_hi, pieces)),
    ]
    vm = pl.BlockSpec(memory_space=pltpu.VMEM)
    sds = jax.ShapeDtypeStruct
    first, second, gain, bias, proto_t, loss = pl.pallas_call(
        functools.partial(step_kernel, nb, npr, pieces, tile_h, tile_k),
        out_shape=[
            sds((share, hid_n), F32), sds((share_h, emb_n), F32), sds((1, hid_n), F32),
            sds((1, hid_n), F32), sds((emb_share, cols), F32), sds((1, 128), F32),
        ],
        in_specs=[vm] * 7,
        out_specs=[vm] * 6,
        scratch_shapes=scratch,
        compiler_params=pltpu.CompilerParams(
            collective_id=0, has_side_effects=True, vmem_limit_bytes=60 * 1024 * 1024),
    )(features, w_first, bn_gain[None], bn_bias[None], w_second, prototypes, pair[None])
    return first, second, gain[0], bias[0], proto_t.T, loss[0, 0]


def solution(mesh):
    return jax.shard_map(
        local,
        mesh=mesh,
        in_specs=(P(("batch", "proto"), None), P(), P(), P(), P(), P("proto", None), P("batch")),
        out_specs=(
            P(("batch", "proto"), None),
            P(("batch", "proto"), None),
            P(),
            P(),
            P("proto", "batch"),
            P(),
        ),
        check_vma=False,
    )
```

```python
import functools

import jax
import jax.numpy as jnp
from jax import lax
from jax.experimental import pallas as pl
from jax.experimental.pallas import tpu as pltpu
from jax.sharding import PartitionSpec as P

ITERS = 3
MESH = pl.DeviceIdType.MESH
F32 = jnp.float32
BF16 = jnp.bfloat16
GELU_C = 0.7978845608028654
GELU_A = 0.044715


def nn(a, b):
    return jnp.dot(a, b, preferred_element_type=F32)


def nt(a, b):
    return lax.dot_general(a, b, (((1,), (1,)), ((), ())), preferred_element_type=F32)


def inner_sizes(nb, npr):
    inner = 2 ** ((nb.bit_length() - 1) // 2)
    return inner if nb % inner == 0 else 1, 2 if npr % 2 == 0 else 1


def step_kernel(
    nb, npr, pieces, tile_h, tile_k,
    feat, w1_far, gain, bias, w2_far, protos_far, pair,
    o_first, o_second, o_gain, o_bias, o_proto, o_loss,
    pre, hidden, feat_t, hid_t, feat_g, hid_g, dshift,
    st_p, st_b, emb_all, emb_t, pb, pscale, kern, col_x, row_x, rmat, amat, cvec,
    ep, rpm, softm, logm, lossv, dacc, d_x, pterm, pt_x, de_g, gb_p, gb_b, dp_g, rs_src, rs_x,
    w1, w2, protos, s_w1, s_in,
    rs2_src, rs2_x, stats, protos_t, pt_y, pt_x2, rs_y, rs_x2,
    s_st_p, s_st_b, s_feat, s_hid, s_emb, s_col, s_row, s_d, s_pt, s_de, s_gb_p, s_gb_b,
    s_dph, s_dpl, s_dpf, s_rs, s_rs2, s_pt2, s_rsb,
):
    me_b = lax.axis_index("batch")
    me_p = lax.axis_index("proto")
    rows, hid_n = pre.shape
    d_in = feat.shape[1]
    block = rows * npr
    emb_n = w2.shape[1]
    cols = protos.shape[0]
    tiles = hid_n // tile_h
    loads = [pltpu.make_async_copy(
        w1_far.at[:, pl.ds(i * tile_h, tile_h)], w1.at[i], s_w1.at[i]) for i in range(tiles)]
    load_protos = pltpu.make_async_copy(protos_far, protos, s_in.at[0])
    load_w2 = pltpu.make_async_copy(w2_far, w2, s_in.at[1])
    for load in loads + [load_protos, load_w2]:
        load.start()
    total = block * nb
    b_lo, p_lo = inner_sizes(nb, npr)
    b_hi, p_hi = nb // b_lo, npr // p_lo
    bh, bl, ph, pq = me_b // b_lo, me_b % b_lo, me_p // p_lo, me_p % p_lo
    size = {"batch": nb, "proto": npr, "b_lo": b_lo, "b_hi": b_hi, "p_lo": p_lo, "p_hi": p_hi}
    me = {"batch": me_b, "proto": me_p, "b_lo": bl, "b_hi": bh, "p_lo": pq, "p_hi": ph}
    place = {
        "batch": lambda i: {"batch": i}, "proto": lambda i: {"proto": i},
        "b_lo": lambda i: {"batch": bh * b_lo + i}, "b_hi": lambda i: {"batch": i * b_lo + bl},
        "p_lo": lambda i: {"proto": ph * p_lo + i}, "p_hi": lambda i: {"proto": i * p_lo + pq},
    }

    def peer(axis, d):
        return lax.rem(me[axis] + d, size[axis])

    def copies(axis, src, dst, sems, pick=lambda sem, k, d: sem.at[k, d]):
        out = []
        n = size[axis]
        for d in range(1, n):
            to, frm = lax.rem(me[axis] + d, n), lax.rem(me[axis] + n - d, n)
            send = pltpu.make_async_remote_copy(
                src_ref=src(to), dst_ref=dst(me[axis]), send_sem=pick(sems, 0, d),
                recv_sem=pick(sems, 1, d), device_id=place[axis](to), device_id_type=MESH)
            recv = pltpu.make_async_remote_copy(
                src_ref=src(to), dst_ref=dst(frm), send_sem=pick(sems, 0, d),
                recv_sem=pick(sems, 1, d), device_id=place[axis](to), device_id_type=MESH)
            out.append((send, recv))
        return out

    def start(cs):
        for send, _ in cs:
            send.start()
        return cs

    def recv(cs):
        for _, r in cs:
            r.wait_recv()

    def sent(cs):
        for s, _ in cs:
            s.wait_send()

    barrier = pltpu.get_barrier_semaphore()
    for axis in ("batch", "proto"):
        for d in range(1, size[axis]):
            pl.semaphore_signal(barrier, inc=1, device_id={axis: peer(axis, d)}, device_id_type=MESH)

    pending = []

    for i in range(tiles):
        at = slice(i * tile_h, (i + 1) * tile_h)
        at2 = slice(hid_n + i * tile_h, hid_n + (i + 1) * tile_h)
        loads[i].wait()
        x = nn(feat[...], w1[i])
        pre[:, at] = x
        st_p[me_p, :, at] = jnp.sum(x, axis=0, keepdims=True)
        st_p[me_p, :, at2] = jnp.sum(x * x, axis=0, keepdims=True)

    pl.semaphore_wait(barrier, nb + npr - 2)
    c_sp = start(copies("proto", lambda to: st_p.at[me_p], lambda f: st_p.at[f], s_st_p))
    share = d_in // (nb * npr)
    share_h = hid_n // (nb * npr)

    def transpose_to(dst, x):
        dst[...] = jnp.transpose(x.astype(F32)).astype(BF16).reshape(dst.shape)

    transpose_to(feat_t, feat[...])

    def spread(src, dst, sems, width):
        own = pl.ds(pl.multiple_of(me_p * rows, rows), rows)
        for b in range(nb):
            dst[pl.ds(b * width, width), own] = src[b, me_p]
        cs = []
        for b in range(nb):
            cs += start(copies(
                "proto", lambda to, b=b: src.at[b, to],
                lambda f, b=b: dst.at[pl.ds(b * width, width), pl.ds(pl.multiple_of(f * rows, rows), rows)],
                sems, lambda sem, k, d, b=b: sem.at[k, d, b]))
        return cs

    recv(c_sp)
    acc = st_p[0]
    for p in range(1, npr):
        acc = acc + st_p[p]
    st_b[me_b] = acc
    c_sb = start(copies("batch", lambda to: st_b.at[me_b], lambda f: st_b.at[f], s_st_b))
    pending += [c_sp, c_sb]
    c_feat = spread(feat_t, feat_g, s_feat, share)
    pending.append(c_feat)

    load_protos.wait()
    load_w2.wait()

    @pl.loop(0, cols // tile_k)
    def _(j):
        at = pl.ds(pl.multiple_of(j * tile_k, tile_k), tile_k)
        x = jnp.transpose(protos[at, :].astype(F32))
        protos_t[:, at] = x.astype(BF16)
        sc = lax.rsqrt(jnp.sum(x * x, axis=0, keepdims=True) + 1e-06)
        pscale[:, at] = sc
        pb[:, at] = (x * sc).astype(BF16)

    recv(c_sb)
    acc = st_b[0]
    for b in range(1, nb):
        acc = acc + st_b[b]
    mean = acc[:, :hid_n] / total
    inv_std = lax.rsqrt(acc[:, hid_n:] / total - mean * mean + 1e-05)
    stats[:, :hid_n] = mean
    stats[:, hid_n:] = inv_std

    def norm_tile(at, at2):
        return (pre[:, at] - stats[:, at]) * stats[:, at2]

    dacc[0:rows, :] = jnp.zeros((rows, emb_n), F32)

    @pl.loop(0, hid_n // tile_h)
    def _(j):
        at = pl.ds(pl.multiple_of(j * tile_h, tile_h), tile_h)
        at2 = pl.ds(pl.multiple_of(hid_n + j * tile_h, tile_h), tile_h)
        x = norm_tile(at, at2) * gain[:, at] + bias[:, at]
        t = jnp.tanh(GELU_C * (x + GELU_A * (x * x * x)))
        h = (x * (0.5 * (1.0 + t))).astype(BF16)
        hidden[:, at] = h
        dacc[0:rows, :] += nn(h, w2[at, :])

    embed = dacc[0:rows, :]
    escale = lax.rsqrt(jnp.sum(embed * embed, axis=1, keepdims=True) + 1e-06)
    unit = embed * escale
    mine = pl.ds(pl.multiple_of(me_p * rows, rows), rows)
    emb_all[mine, :] = unit.astype(BF16)
    c_emb = start(copies(
        "proto", lambda to: emb_all.at[mine],
        lambda f: emb_all.at[pl.ds(pl.multiple_of(f * rows, rows), rows)], s_emb))
    pending.append(c_emb)
    transpose_to(hid_t, hidden[...])
    c_hid = spread(hid_t, hid_g, s_hid, share_h)
    pending.append(c_hid)
    hits = lax.broadcasted_iota(jnp.int32, (block, block), 0) == (pair[...] - me_b * block)
    recv(c_emb)

    amat[...] = jnp.zeros_like(amat)

    @pl.loop(0, cols // tile_k)
    def _(j):
        at = pl.ds(pl.multiple_of(j * tile_k, tile_k), tile_k)
        e = jnp.exp(10.0 * nn(emb_all[...], pb[:, at]))
        part = e[:, 0:128]
        for q in range(1, tile_k // 128):
            part = part + e[:, q * 128:(q + 1) * 128]
        amat[...] += part
        k = e * e
        kern[:, at] = k
        col_x[0, me_b, :, at] = jnp.sum(k, axis=0, keepdims=True)

    soft_row = jnp.sum(jnp.transpose(amat[...]), axis=0, keepdims=True)

    lanes = 128
    chunk = 64
    for it in range(ITERS):
        if it > 0:
            @pl.loop(0, cols // lanes)
            def _(j):
                at = pl.ds(pl.multiple_of(j * lanes, lanes), lanes)
                col_x[it, me_b, :, at] = jnp.sum(kern[:, at] * rmat[...], axis=0, keepdims=True)
        c = start(copies("batch", lambda to: col_x.at[it, me_b], lambda f: col_x.at[it, f],
                         s_col, lambda sem, k, d: sem.at[it, k, d]))
        pending.append(c)
        recv(c)
        acc = col_x[it, 0]
        for b in range(1, nb):
            acc = acc + col_x[it, b]
        cvec[...] = 1.0 / acc

        @pl.loop(0, block // chunk)
        def _(i):
            at = pl.ds(pl.multiple_of(i * chunk, chunk), chunk)
            a = kern[at, 0:lanes] * cvec[:, 0:lanes]
            for q in range(1, cols // lanes):
                a = a + kern[at, q * lanes:(q + 1) * lanes] * cvec[:, q * lanes:(q + 1) * lanes]
            amat[at, :] = a

        row_x[it, me_p, :, 0:block] = jnp.sum(jnp.transpose(amat[...]), axis=0, keepdims=True)
        row_x[it, me_p, :, block:] = soft_row
        c = start(copies("proto", lambda to: row_x.at[it, me_p], lambda f: row_x.at[it, f],
                         s_row, lambda sem, k, d: sem.at[it, k, d]))
        pending.append(c)
        recv(c)
        acc = row_x[it, 0]
        for p in range(1, npr):
            acc = acc + row_x[it, p]
        r_row = 1.0 / acc[:, :block]
        if it < ITERS - 1:
            rmat[...] = jnp.transpose(jnp.broadcast_to(r_row, (lanes, block)))
        else:
            soft = jnp.transpose(jnp.broadcast_to(acc[:, block:], (lanes, block)))
            softm[...] = 10.0 / soft
            logm[...] = jnp.log(soft)
            rp = jnp.sum(jnp.where(hits, r_row, 0.0), axis=1, keepdims=True)
            rpm[...] = jnp.broadcast_to(rp, (block, lanes))

    ep[...] = nn(jnp.where(hits, 1.0, 0.0).astype(BF16), emb_all[...]).astype(BF16)
    emb_t[...] = jnp.transpose(emb_all[...].astype(F32)).astype(BF16)
    dacc[...] = jnp.zeros_like(dacc)
    lossv[...] = jnp.zeros_like(lossv)
    reps = tile_k // lanes

    def wide(ref):
        return jnp.concatenate([ref[...]] * reps, axis=1)

    emb_share = emb_n // nb
    group = cols // pieces

    def tile_step(g, j):
        at = pl.ds(pl.multiple_of(g * group + j * tile_k, tile_k), tile_k)
        at_g = pl.ds(pl.multiple_of(j * tile_k, tile_k), tile_k)
        s = 10.0 * nn(emb_all[...], pb[:, at])
        goal = jnp.exp(20.0 * nn(ep[...], pb[:, at])) * wide(rpm) * cvec[:, at]
        lossv[...] -= jnp.sum(goal * (s - wide(logm)), axis=0, keepdims=True)
        gs = (jnp.exp(s) * wide(softm) - 10.0 * goal).astype(BF16)
        dacc[...] += nt(gs, pb[:, at])
        acc = nn(emb_t[...], gs)
        sc = pscale[:, at]
        up = protos_t[:, at].astype(F32) * sc
        term = (acc - up * jnp.sum(up * acc, axis=0, keepdims=True)) * sc
        pterm[g, :, :, :, at_g] = term.astype(BF16).reshape(b_hi, b_lo, emb_share, tile_k)

    c_pt = []
    for g in range(pieces):
        @pl.loop(0, group // tile_k)
        def _(j):
            tile_step(g, j)

        c_pt.append(start(copies(
            "b_lo", lambda to: pterm.at[g, :, to], lambda f: pt_x.at[g, f],
            s_pt, lambda sem, k, d: sem.at[k, d, g])))

    c_d = start(copies(
        "proto", lambda to: dacc.at[pl.ds(pl.multiple_of(to * rows, rows), rows)],
        lambda f: d_x.at[f], s_d))
    pending += [c_d] + c_pt
    c_pt2 = []

    def forward_pt(g):
        pt_x[g, bl] = pterm[g, :, bl]
        recv(c_pt[g])
        for h in range(b_hi):
            acc = pt_x[g, 0, h].astype(F32)
            for l in range(1, b_lo):
                acc = acc + pt_x[g, l, h].astype(F32)
            pt_y[g, h] = acc.astype(BF16)
        c_pt2.append(start(copies(
            "b_hi", lambda to: pt_y.at[g, to], lambda f: pt_x2.at[g, f],
            s_pt2, lambda sem, k, d: sem.at[k, d, g])))

    half = pieces // 2
    for g in range(half):
        forward_pt(g)
    d_x[me_p] = dacc[mine, :]
    recv(c_d)
    d_unit = d_x[0]
    for p in range(1, npr):
        d_unit = d_unit + d_x[p]
    d_embed = ((d_unit - unit * jnp.sum(unit * d_unit, axis=1, keepdims=True)) * escale).astype(BF16)
    de_g[mine, :] = d_embed
    c_de = start(copies(
        "proto", lambda to: de_g.at[mine],
        lambda f: de_g.at[pl.ds(pl.multiple_of(f * rows, rows), rows)], s_de))
    pending.append(c_de)

    @pl.loop(0, hid_n // tile_h)
    def _(j):
        at = pl.ds(pl.multiple_of(j * tile_h, tile_h), tile_h)
        at2 = pl.ds(pl.multiple_of(hid_n + j * tile_h, tile_h), tile_h)
        dh = nt(de_g[mine, :], w2[at, :])
        nrm = norm_tile(at, at2)
        x = nrm * gain[:, at] + bias[:, at]
        t = jnp.tanh(GELU_C * (x + GELU_A * (x * x * x)))
        slope = 0.5 * (1.0 + t) + 0.5 * x * (1.0 - t * t) * (GELU_C * (1.0 + 3.0 * GELU_A * (x * x)))
        ds = slope * dh
        dshift[:, at] = ds
        gb_p[me_p, :, at] = jnp.sum(ds * nrm, axis=0, keepdims=True)
        gb_p[me_p, :, at2] = jnp.sum(ds, axis=0, keepdims=True)

    gb_p[me_p, :, 2 * hid_n:] = jnp.broadcast_to(jnp.sum(lossv[...], axis=1, keepdims=True), (1, lanes))
    c_gp = start(copies("proto", lambda to: gb_p.at[me_p], lambda f: gb_p.at[f], s_gb_p))
    for g in range(half, pieces):
        forward_pt(g)
    pending += c_pt2
    recv(c_gp)
    acc = gb_p[0]
    for p in range(1, npr):
        acc = acc + gb_p[p]
    gb_b[me_b] = acc
    c_gb = start(copies("batch", lambda to: gb_b.at[me_b], lambda f: gb_b.at[f], s_gb_b))
    pending += [c_gp, c_gb]

    recv(c_hid)
    recv(c_de)
    rs2_src[...] = nn(hid_g[...], de_g[...]).astype(BF16)
    c_rs2 = start(copies(
        "batch", lambda to: rs2_src.at[pl.ds(pl.multiple_of(to * share_h, share_h), share_h)],
        lambda f: rs2_x.at[f], s_rs2))
    pending.append(c_rs2)
    rs2_x[me_b] = rs2_src[pl.ds(pl.multiple_of(me_b * share_h, share_h), share_h), :]
    recv(c_feat)

    recv(c_gb)
    acc = gb_b[0]
    for b in range(1, nb):
        acc = acc + gb_b[b]
    o_gain[...] = acc[:, :hid_n]
    o_bias[...] = acc[:, hid_n:2 * hid_n]
    o_loss[...] = acc[:, 2 * hid_n:] / total

    width = hid_n // pieces

    def rows_of(q, p):
        return dp_g.at[q, pl.ds(pl.multiple_of(p * rows, rows), rows)]

    c_far, c_near = [], []
    for q in range(pieces):
        at = slice(q * width, (q + 1) * width)
        at2 = slice(hid_n + q * width, hid_n + (q + 1) * width)
        nrm = norm_tile(at, at2)
        dp = gain[:, at] * stats[:, at2] * (
            dshift[:, at] - o_bias[:, at] / total - nrm * (o_gain[:, at] / total))
        dp_g[q, mine, :] = dp.astype(BF16)
        c_far.append(start(copies(
            "p_hi", lambda to: rows_of(q, me_p), lambda f: rows_of(q, f * p_lo + pq),
            s_dph, lambda sem, k, d: sem.at[k, d, q])))
        c_near.append(start(copies(
            "p_lo", lambda to: rows_of(q, me_p), lambda f: rows_of(q, ph * p_lo + f),
            s_dpl, lambda sem, k, d: sem.at[k, d, q])))

    def pass_on(q):
        out = []
        for e in range(1, p_hi):
            recv(c_far[q][e - 1:e])
            frm = lax.rem(ph + p_hi - e, p_hi)
            out += start(copies(
                "p_lo", lambda to: rows_of(q, frm * p_lo + pq), lambda f: rows_of(q, frm * p_lo + f),
                s_dpf, lambda sem, k, d: sem.at[k, d, e, q]))
        return out

    c_rs, c_rsb = [], []

    def forward_rs(q):
        rs_x[q, bl] = rs_src[q, :, bl]
        recv(c_rs[q])
        for h in range(b_hi):
            acc = rs_x[q, 0, h].astype(F32)
            for l in range(1, b_lo):
                acc = acc + rs_x[q, l, h].astype(F32)
            rs_y[q, h] = acc.astype(BF16)
        c_rsb.append(start(copies(
            "b_hi", lambda to: rs_y.at[q, to], lambda f: rs_x2.at[q, f],
            s_rsb, lambda sem, k, d: sem.at[k, d, q])))

    c_fwd = [pass_on(0)]
    for q in range(pieces):
        recv(c_near[q])
        recv(c_fwd[q])
        rs_src[q] = nn(feat_g[...], dp_g[q]).astype(BF16).reshape(b_hi, b_lo, share, width)
        c_rs.append(start(copies(
            "b_lo", lambda to: rs_src.at[q, :, to], lambda f: rs_x.at[q, f],
            s_rs, lambda sem, k, d: sem.at[k, d, q])))
        if q + 1 < pieces:
            c_fwd.append(pass_on(q + 1))
        if q > 0:
            forward_rs(q - 1)
    forward_rs(pieces - 1)
    pending += c_far + c_near + c_fwd + c_rs + c_rsb

    for g in range(pieces):
        pt_x2[g, bh] = pt_y[g, bh]
        recv(c_pt2[g])
        acc = pt_x2[g, 0].astype(F32)
        for h in range(1, b_hi):
            acc = acc + pt_x2[g, h].astype(F32)
        o_proto[:, g * group:(g + 1) * group] = acc

    recv(c_rs2)
    acc = rs2_x[0].astype(F32)
    for b in range(1, nb):
        acc = acc + rs2_x[b].astype(F32)
    o_second[...] = acc
    for q in range(pieces):
        rs_x2[q, bh] = rs_y[q, bh]
        recv(c_rsb[q])
        acc = rs_x2[q, 0].astype(F32)
        for h in range(1, b_hi):
            acc = acc + rs_x2[q, h].astype(F32)
        o_first[:, q * width:(q + 1) * width] = acc
    for cs in pending:
        sent(cs)


def hand_out(first, second, gain, bias, proto, loss, o_first, o_second, o_gain, o_bias, o_proto, o_loss):
    o_first[...] = first[...]
    o_second[...] = second[...]
    o_gain[...] = gain[0, :]
    o_bias[...] = bias[0, :]
    o_proto[...] = proto[...]
    o_loss[...] = loss[...]


def local(features, w_first, bn_gain, bn_bias, w_second, prototypes, pair):
    nb = lax.axis_size("batch")
    npr = lax.axis_size("proto")
    rows, d_in = features.shape
    hid_n, emb_n = w_second.shape
    cols = prototypes.shape[0]
    block = rows * npr
    share, share_h, emb_share = d_in // (nb * npr), hid_n // (nb * npr), emb_n // nb
    pieces = 4
    width, group = hid_n // pieces, cols // pieces
    b_lo, p_lo = inner_sizes(nb, npr)
    b_hi, p_hi = nb // b_lo, npr // p_lo
    tile_h = min(512, hid_n)
    tile_k = 256
    dma = pltpu.SemaphoreType.DMA
    V = pltpu.VMEM
    scratch = [
        V((rows, hid_n), F32), V((rows, hid_n), BF16),
        V((nb, npr, share, rows), BF16), V((nb, npr, share_h, rows), BF16),
        V((nb * share, block), BF16), V((nb * share_h, block), BF16),
        V((rows, hid_n), F32),
        V((npr, 1, 2 * hid_n), F32), V((nb, 1, 2 * hid_n), F32),
        V((block, emb_n), BF16), V((emb_n, block), BF16),
        V((emb_n, cols), BF16), V((1, cols), F32), V((block, cols), F32),
        V((ITERS, nb, 1, cols), F32), V((ITERS, npr, 1, 2 * block), F32),
        V((block, 128), F32), V((block, 128), F32), V((1, cols), F32),
        V((block, emb_n), BF16), V((block, 128), F32), V((block, 128), F32), V((block, 128), F32),
        V((1, tile_k), F32), V((block, emb_n), F32), V((npr, rows, emb_n), F32),
        V((pieces, b_hi, b_lo, emb_share, group), BF16), V((pieces, b_lo, b_hi, emb_share, group), BF16), V((block, emb_n), BF16),
        V((npr, 1, 2 * hid_n + 128), F32), V((nb, 1, 2 * hid_n + 128), F32),
        V((pieces, block, width), BF16),
        V((pieces, b_hi, b_lo, share, width), BF16), V((pieces, b_lo, b_hi, share, width), BF16),
        V((hid_n // tile_h, d_in, tile_h), BF16), V((hid_n, emb_n), BF16), V((cols, emb_n), BF16),
        dma((hid_n // tile_h,)), dma((2,)),
        V((nb * share_h, emb_n), BF16), V((nb, share_h, emb_n), BF16),
        V((1, 2 * hid_n), F32), V((emb_n, cols), BF16),
        V((pieces, b_hi, emb_share, group), BF16), V((pieces, b_hi, emb_share, group), BF16),
        V((pieces, b_hi, share, width), BF16), V((pieces, b_hi, share, width), BF16),
        dma((2, npr)), dma((2, nb)), dma((2, npr, nb)), dma((2, npr, nb)), dma((2, npr)),
        dma((ITERS, 2, nb)), dma((ITERS, 2, npr)), dma((2, npr)), dma((2, b_lo, pieces)), dma((2, npr)),
        dma((2, npr)), dma((2, nb)), dma((2, p_hi, pieces)), dma((2, p_lo, pieces)),
        dma((2, p_lo, p_hi, pieces)), dma((2, b_lo, pieces)), dma((2, nb)),
        dma((2, b_hi, pieces)), dma((2, b_hi, pieces)),
    ]
    vm = pl.BlockSpec(memory_space=pltpu.VMEM)
    far = pl.BlockSpec(memory_space=pl.ANY)
    sds = jax.ShapeDtypeStruct
    first, second, gain, bias, proto_t, loss = pl.pallas_call(
        functools.partial(step_kernel, nb, npr, pieces, tile_h, tile_k),
        out_shape=[
            sds((share, hid_n), F32), sds((share_h, emb_n), F32), sds((1, hid_n), F32),
            sds((1, hid_n), F32), sds((emb_share, cols), F32), sds((1, 128), F32),
        ],
        in_specs=[vm, far, vm, vm, far, far, vm],
        out_specs=[vm] * 6,
        scratch_shapes=scratch,
        compiler_params=pltpu.CompilerParams(
            collective_id=0, has_side_effects=True, vmem_limit_bytes=60 * 1024 * 1024),
    )(features, w_first, bn_gain[None], bn_bias[None], w_second, prototypes, pair[None])
    first, second, gain, bias, proto_t, loss = pl.pallas_call(
        hand_out,
        out_shape=[
            sds((share, hid_n), F32), sds((share_h, emb_n), F32), sds((hid_n,), F32), sds((hid_n,), F32),
            sds((emb_share, cols), F32), sds((1, 128), F32),
        ],
        in_specs=[vm] * 6,
        out_specs=[vm] * 6,
    )(first, second, gain, bias, proto_t, loss)
    return first, second, gain, bias, proto_t.T, loss[0, 0]


def solution(mesh):
    return jax.shard_map(
        local,
        mesh=mesh,
        in_specs=(P(("batch", "proto"), None), P(), P(), P(), P(), P("proto", None), P("batch")),
        out_specs=(
            P(("batch", "proto"), None),
            P(("batch", "proto"), None),
            P(),
            P(),
            P("proto", "batch"),
            P(),
        ),
        check_vma=False,
    )
```
